32 devices in a mesh: groups: 2 (over y), dp: 4 (over z), tensor: 4 (over x, core).
Axes of the slice: x: 2, y: 2, z: 4, core: 2. Of those that a mesh axis runs over, the one named last changes fastest.
Arguments:
- stored_input: bfloat16 [8192, 8192], P(('groups', 'dp'), 'tensor'), parts along dimension 0, may hold values from -6 to 6
- output_gradient: bfloat16 [8192, 2048], P(('groups', 'dp'), 'tensor'), parts along dimension 0, may hold values from -3 to 3
- frozen_key_value: bfloat16 [8192, 2048], P('tensor'), may hold values from -0.0625 to 0.0625
- adapter_down_weight: bfloat16 [24, 32, 8192], P('groups', None, 'tensor'), parts along dimension 0, may hold values from -0.0625 to 0.0625
- adapter_up_weight: bfloat16 [24, 32, 2048], P('groups', None, 'tensor'), parts along dimension 0, may hold values from -0.125 to 0.125
- token_tenant: int32 [8192, 1], P(('groups', 'dp')), parts along dimension 0, may hold values from 0 to 11; in each aligned block of 1024 rows (0 to 1023, 1024 to 2047, ...) at most 258 rows name the same one
- adapter_position: int32 [24], P('groups'), parts along dimension 0, may hold values from 0 to 11, each once
Outputs:
- input_gradient: bfloat16 [8192, 8192], P(('groups', 'dp'), 'tensor'), parts along dimension 0
- down_grad: float32 [24, 32, 8192], P(('groups', 'dp'), None, 'tensor'), parts along dimension 0
- up_grad: float32 [24, 32, 2048], P(('groups', 'dp'), None, 'tensor'), parts along dimension 0
The draws below stay inside these ranges and needn't reach their ends.
There are 2 independent parts, one for each index of `groups`. The reference program is written for one: setup_inputs(seed, part) draws one part's arguments, and reference() takes and returns one part's arrays. A program takes and returns all parts, laid end to end along the dimension named above; an argument that names none is the same for every part. Nothing has to cross between parts.
Inputs may be any that keep to these rules, and one draw needn't show every extreme that they name: `token_tenant`: among the tokens of one index of dp no adapter is named more than 258 times, a bound that some block reaches; every adapter is named by some token of the part. `adapter_position`: A permutation: each slot holds one adapter.
All inputs are finite; a program needn't handle non-finite values.
Results may differ from the reference program's by a relative error of at most 0.0029.
Values may be sent and summed in bfloat16 or wider, within the bound.
A program may use at most 192 MiB of HBM per device.

```python
import math
import jax
import jax.numpy as jnp
import numpy as np
from jax import lax

MODEL_WIDTH = 8192
KEY_VALUE_WIDTH = 2048
ADAPTER_RANK = 32
TENANT_ADAPTERS = 12
TOK_DEV = 1024
PACKED_TOKENS = 4096
CAP = 258
N_DP = 4


def block_levels(stream_key, extent, shards, smallest, high):
    factor_of, own = 1.0, jax.random.fold_in(stream_key, 6)
    for axis_at, shards_of in shards:
        steps = jnp.exp(jax.random.uniform(jax.random.fold_in(own, axis_at), (shards_of,), jnp.float32, smallest / len(shards), high / len(shards)))
        factor_of = factor_of * jnp.repeat(steps, extent[axis_at] // shards_of).reshape([-1 if axis == axis_at else 1 for axis in range(len(extent))])
    return factor_of


def routed_block(stream_key, own, number, rows, number_of, top, reach, slope):
    sequence = jax.random.permutation(stream_key, number_of)
    crowded, usual = load_shares(number_of, rows * top, reach, slope, True), load_shares(number_of, rows * top, reach, slope, False)
    places = jnp.arange(number_of)

    def named(tallies, rotation):
        used = int((tallies > 0).sum())
        fixed = max(1, used // 4)
        shifted = fixed + (places - fixed + rotation * (used - fixed)) % max(1, number_of - fixed)
        return jnp.zeros((number_of,), jnp.int32).at[sequence[jnp.where(places < fixed, places, shifted)]].set(jnp.asarray(tallies, jnp.int32))

    tallies = jnp.where(number % 4 == 0, named(crowded, number // 4), named(usual, number - number // 4 - 1))
    mixed = jax.random.permutation(jax.random.fold_in(own, 3), number_of)
    source_of, sink = mixed[0:number_of // 2 * 2:2], mixed[1:number_of // 2 * 2:2]
    room = jnp.minimum(tallies[source_of] - 1, reach - tallies[sink]) // 2
    room = jnp.where((source_of == sequence[0]) | (sink == sequence[0]) | (tallies[sink] == 0), 0, jnp.maximum(room, 0))
    shifted = jax.random.randint(jax.random.fold_in(own, 4), (number_of // 2,), 0, 1 << 20) % (room + 1)
    tallies = tallies.at[source_of].add(-shifted).at[sink].add(shifted)
    labels = jnp.searchsorted(jnp.cumsum(tallies), jnp.arange(rows * top), side="right").astype(jnp.int32)
    listing = labels.reshape(top, rows).T
    listing = listing[jax.random.permutation(jax.random.fold_in(own, 1), rows)]
    rotation = jax.random.randint(jax.random.fold_in(own, 2), (rows, 1), 0, top)
    return jnp.take_along_axis(listing, (jnp.arange(top)[None, :] + rotation) % top, axis=1)


def load_shares(number_of, total, most, slope, full):
    portions = [(1 << 20) // math.isqrt(rank ** slope) + 1 for rank in range(1, number_of + 1)]
    largest = most if full else min(most, max(-(-total // number_of), total * portions[0] // sum(portions)))
    least = 1 if total - largest >= number_of - 1 else 0
    holding, surplus = [largest] + [least] * (number_of - 1), total - largest - least * (number_of - 1)
    while surplus > 0:
        candidates = [i for i in range(1, number_of) if holding[i] < largest] or [i for i in range(1, number_of) if holding[i] < most]
        whole, budget = sum([portions[i] for i in candidates]), surplus
        for i in candidates:
            extra = min(most - holding[i], max(1, budget * portions[i] // whole), surplus)
            holding[i] = holding[i] + extra
            surplus = surplus - extra
    return np.array(holding)


def scatter_about(rng, dims, width, limit, pieces=(), kind=jnp.bfloat16):
    values = width * jax.random.normal(rng, dims, jnp.float32)
    if pieces:
        values = values * block_levels(rng, dims, pieces, -0.22, 0.18)
    return jnp.clip(values, -limit, limit).astype(kind)


def setup_inputs(seed: int = 0, part: int = 0) -> dict:
    arg_keys = jax.random.split(jax.random.key(seed), 8)
    own_keys = jax.random.split(jax.random.fold_in(arg_keys[7], part), 8)
    stored_input = scatter_about(own_keys[0], (PACKED_TOKENS, MODEL_WIDTH), 1.0, 6.0, ((0, 4), (1, 4)))
    output_gradient = scatter_about(own_keys[1], (PACKED_TOKENS, KEY_VALUE_WIDTH), 0.5, 3.0, ((0, 4), (1, 4)))
    frozen_key_value = scatter_about(arg_keys[2], (MODEL_WIDTH, KEY_VALUE_WIDTH), MODEL_WIDTH ** -0.5, 0.0625, ((0, 4),))
    adapter_down_weight = scatter_about(own_keys[3], (TENANT_ADAPTERS, ADAPTER_RANK, MODEL_WIDTH), MODEL_WIDTH ** -0.5, 0.0625, ((2, 4),))
    adapter_up_weight = scatter_about(own_keys[4], (TENANT_ADAPTERS, ADAPTER_RANK, KEY_VALUE_WIDTH), KEY_VALUE_WIDTH ** -0.5, 0.125, ((2, 4),))
    token_tenant_keys = jax.random.split(jax.random.fold_in(own_keys[5], 1), PACKED_TOKENS // TOK_DEV)
    token_tenant_turns = jax.random.permutation(jax.random.fold_in(own_keys[5], 3), PACKED_TOKENS // TOK_DEV)
    token_tenant = jax.vmap(lambda own, number: routed_block(jax.random.fold_in(own_keys[5], 2), own, number, TOK_DEV, TENANT_ADAPTERS, 1, CAP, 2))(token_tenant_keys, token_tenant_turns).reshape((PACKED_TOKENS, 1))
    adapter_position = jax.random.permutation(own_keys[6], TENANT_ADAPTERS).astype(jnp.int32)
    return {"stored_input": stored_input, "output_gradient": output_gradient, "frozen_key_value": frozen_key_value, "adapter_down_weight": adapter_down_weight, "adapter_up_weight": adapter_up_weight, "token_tenant": token_tenant, "adapter_position": adapter_position}


def reference(stored_input, output_gradient, frozen_key_value, adapter_down_weight, adapter_up_weight, token_tenant, adapter_position):
    adapter_ids = token_tenant[:, 0].astype(jnp.int32)
    longest = CAP * N_DP
    sorted_ids = jnp.argsort(adapter_ids, stable=True).astype(jnp.int32)
    counts = jnp.sum((adapter_ids[None, :] == jnp.arange(TENANT_ADAPTERS, dtype=jnp.int32)[:, None]).astype(jnp.int32), axis=1)
    starts = (jnp.cumsum(counts) - counts).astype(jnp.int32)
    padded = jnp.concatenate([sorted_ids, jnp.zeros((longest,), jnp.int32)])

    def adapter_gradients(running_total, adapter_number):
        selected_rows = lax.dynamic_slice(padded, (starts[adapter_number],), (longest,))
        in_range = (jnp.arange(longest, dtype=jnp.int32) < counts[adapter_number])[:, None]
        input_rows = stored_input[selected_rows]
        gradient_rows = output_gradient[selected_rows]
        projected_input = jnp.dot(input_rows, adapter_down_weight[adapter_number].T, preferred_element_type=jnp.float32)
        projected_gradient = jnp.dot(gradient_rows, adapter_up_weight[adapter_number].T, preferred_element_type=jnp.float32)
        low_u = jnp.where(in_range, projected_input, 0.0).astype(jnp.bfloat16)
        rank_gradient = jnp.where(in_range, projected_gradient, 0.0).astype(jnp.bfloat16)
        down_term = jnp.dot(rank_gradient.T, input_rows, preferred_element_type=jnp.float32)
        up_term = jnp.dot(low_u.T, gradient_rows, preferred_element_type=jnp.float32)
        running_total = running_total.at[selected_rows].add(jnp.dot(rank_gradient, adapter_down_weight[adapter_number], preferred_element_type=jnp.float32))
        return running_total, (down_term, up_term)

    adapter_contribution, (down_pieces, up_pieces) = lax.scan(adapter_gradients, jnp.zeros((PACKED_TOKENS, MODEL_WIDTH), jnp.float32), jnp.arange(TENANT_ADAPTERS, dtype=jnp.int32))
    frozen_contribution = jnp.dot(output_gradient, frozen_key_value.T, preferred_element_type=jnp.float32)
    input_gradient = (frozen_contribution + adapter_contribution).astype(jnp.bfloat16)
    down_grad = jnp.zeros_like(down_pieces).at[adapter_position].set(down_pieces)
    up_grad = jnp.zeros_like(up_pieces).at[adapter_position].set(up_pieces)
    return input_gradient, down_grad, up_grad
```

```python
import functools

import jax
import jax.numpy as jnp
from jax import lax
from jax.experimental import pallas as pl
from jax.experimental.pallas import tpu as pltpu
from jax.sharding import PartitionSpec as P

MESH = pl.DeviceIdType.MESH
F32 = jnp.float32
BF16 = jnp.bfloat16
LANES = 128
LAST = (((1,), (1,)), ((), ()))
HALVES = 2
WINDOW = 3


def kernel(nt, nz, rank, x_h, dy_h, w_h, d_h, u_h, tt, pos, ig_h, dg_h, ug_h,
           x, dy, w, d, u, ab, a_t, packed, landed, low, ge, ge_t, ue_t, own, acc, ig,
           r_out, r_in, l_out, l_in, dg, ug,
           load_sem, part_s, part_r, low_s, low_r, dy_s, dy_r, rs_s, rs_r, ls_s, ls_r, out_sem):
    me = lax.axis_index("tensor")
    z = lax.axis_index("dp")
    rows, width = x.shape
    kv = dy.shape[2]
    ar = d.shape[0]
    per = ar // nz
    tiles = ar // LANES
    fold = LANES // rank
    chunk_rows = rows // fold
    down_chunks = width // kv
    chunks = down_chunks + 1
    half = rows // HALVES
    chips = nt // 2
    core = lax.rem(me, 2)
    chip = me // 2
    partner = chip * 2 + 1 - core

    loads = [
        pltpu.make_async_copy(src, dst, load_sem.at[i])
        for i, (src, dst) in enumerate(
            [(u_h, u), (dy_h, dy.at[me]), (d_h, d), (x_h, x), (w_h, w)]
        )
    ]
    for load in loads:
        load.start()

    barrier = pltpu.get_barrier_semaphore()
    for off in range(1, nt):
        pl.semaphore_signal(barrier, inc=1, device_id={"tensor": lax.rem(me + off, nt)},
                            device_id_type=MESH)

    @pl.when(z > 0)
    def _():
        pl.semaphore_signal(barrier, inc=1, device_id={"dp": z - 1}, device_id_type=MESH)

    @pl.when(z < nz - 1)
    def _():
        pl.semaphore_signal(barrier, inc=1, device_id={"dp": z + 1}, device_id_type=MESH)

    for i in range(rows // LANES):
        row = jnp.broadcast_to(tt[i : i + 1, :].astype(F32), (LANES, LANES))
        a_t[:, i * LANES : (i + 1) * LANES] = row[0:8, :]
        ab[i * LANES : (i + 1) * LANES, :] = row.T

    group_of = (lax.broadcasted_iota(jnp.int32, (chunk_rows, LANES), 1) // rank).astype(F32)
    group_t = (lax.broadcasted_iota(jnp.int32, (LANES, chunk_rows), 0) // rank).astype(F32)

    def spread(v):
        step = LANES // 2
        while step >= rank:
            v = v + pltpu.roll(v, step, 1)
            step //= 2
        return v

    def project(kind, source, weight):
        total = jnp.zeros((chunk_rows, LANES), F32)
        for k in range(fold):
            part = lax.dot_general(source(k), weight[...], LAST, preferred_element_type=F32)
            a_k = ab[k * chunk_rows : (k + 1) * chunk_rows, :]
            mine = jnp.zeros((chunk_rows, LANES), F32)
            for j in range(tiles):
                mine = mine + jnp.where(
                    a_k == group_of + float(fold * j), part[:, j * LANES : (j + 1) * LANES], 0.0
                )
            total = jnp.where(group_of == float(k), spread(mine), total)
        packed[kind] = total.reshape(packed.shape[1:])

    def part_copy(kind, off, src_slot, dst_slot):
        return pltpu.make_async_remote_copy(
            src_ref=packed.at[kind, src_slot], dst_ref=landed.at[kind, dst_slot],
            send_sem=part_s.at[kind, off], recv_sem=part_r.at[kind, off],
            device_id={"tensor": lax.rem(me + off, nt)}, device_id_type=MESH)

    def low_copy(kind, off, slot):
        return pltpu.make_async_remote_copy(
            src_ref=low.at[kind, slot], dst_ref=low.at[kind, slot],
            send_sem=low_s.at[kind, off], recv_sem=low_r.at[kind, off],
            device_id={"tensor": lax.rem(me + off, nt)}, device_id_type=MESH)

    def send_parts(kind):
        for off in range(1, nt):
            part_copy(kind, off, lax.rem(me + off, nt), me).start()

    def sum_parts(kind):
        total = packed[kind, me]
        for off in range(1, nt):
            sender = lax.rem(me + nt - off, nt)
            part_copy(kind, off, me, sender).wait_recv()
            total = total + landed[kind, sender]
        low[kind, me] = total.astype(BF16)
        for off in range(1, nt):
            low_copy(kind, off, me).start()

    def get_low(kind):
        for off in range(1, nt):
            low_copy(kind, off, lax.rem(me + nt - off, nt)).wait_recv()
        return low[kind].astype(F32).reshape(chunk_rows, LANES)

    def dy_copy(h, way, slot, to):
        block = dy.at[slot, pl.ds(h * half, half)]
        return pltpu.make_async_remote_copy(
            src_ref=block, dst_ref=block, send_sem=dy_s.at[h, way], recv_sem=dy_r.at[h, way],
            device_id={"tensor": to}, device_id_type=MESH)

    def away(off, side):
        return lax.rem(chip + off + chips, chips) * 2 + side

    loads[0].wait()
    loads[1].wait()
    project(0, lambda k: dy[me, k * chunk_rows : (k + 1) * chunk_rows, :], u)
    neighbours = (z > 0).astype(jnp.int32) + (z < nz - 1).astype(jnp.int32)
    pl.semaphore_wait(barrier, nt - 1 + neighbours)
    send_parts(0)
    for h in range(HALVES):
        dy_copy(h, 0, me, partner).start()
    loads[2].wait()
    loads[3].wait()
    project(1, lambda k: x[k * chunk_rows : (k + 1) * chunk_rows, :], d)
    send_parts(1)
    sum_parts(0)
    sum_parts(1)
    for h in range(HALVES):
        if h == 0:
            for off in range(1, chips):
                dy_copy(h, off, me, away(off, core)).start()

    home = jnp.zeros((8, rows), F32)
    for a in range(ar // rank):
        home = home + jnp.where(a_t[...] == float(a), pos[a].astype(F32), 0.0)

    def expand(kind, out_t, out):
        got = get_low(kind)
        for k in range(fold):
            at = slice(k * chunk_rows, (k + 1) * chunk_rows)
            rep = spread(jnp.where(group_of == float(k), got, 0.0))
            rep_t = rep.T
            home_k = jnp.broadcast_to(home[0:1, at], (LANES, chunk_rows))
            for j in range(tiles):
                cols = slice(j * LANES, (j + 1) * LANES)
                out_t[cols, at] = jnp.where(
                    home_k == group_t + float(fold * j), rep_t, 0.0).astype(BF16)
                if out is not None:
                    out[at, cols] = jnp.where(
                        ab[at, :] == group_of + float(fold * j), rep, 0.0).astype(BF16)

    def term(c):
        if c < down_chunks:
            block = jnp.dot(ge_t[...], x[:, c * kv : (c + 1) * kv], preferred_element_type=F32)
        else:
            block = jnp.dot(ue_t[...], dy[me], preferred_element_type=F32)
        own[c] = block.reshape(nz, per, kv)

    steps = nz - 1
    sends = chunks * steps

    def right_copy(c, j):
        return pltpu.make_async_remote_copy(
            src_ref=r_out.at[c, j], dst_ref=r_in.at[c, j],
            send_sem=rs_s.at[c, j], recv_sem=rs_r.at[c, j],
            device_id={"dp": lax.rem(z + 1, nz)}, device_id_type=MESH)

    def left_copy(c, j):
        return pltpu.make_async_remote_copy(
            src_ref=l_out.at[c, j], dst_ref=l_in.at[c, j],
            send_sem=ls_s.at[c, j], recv_sem=ls_r.at[c, j],
            device_id={"dp": lax.rem(z + nz - 1, nz)}, device_id_type=MESH)

    def one_way(t, index, first, farther, owner_of, copy, out, inn):
        c = index // steps
        j = owner_of(lax.rem(index, steps))

        @pl.when((index >= 0) & (index < sends))
        def _():
            @pl.when(first)
            def _():
                @pl.when(index >= WINDOW)
                def _():
                    back = index - WINDOW
                    copy(back // steps, owner_of(lax.rem(back, steps))).wait_send()

                out[c, j] = own[c, j].astype(out.dtype)
                copy(c, j).start()

            @pl.when(jnp.logical_not(first))
            def _():
                @pl.when(farther(j) | (j == z))
                def _():
                    copy(c, j).wait_recv()

                @pl.when(farther(j))
                def _():
                    out[c, j] = (own[c, j] + inn[c, j].astype(F32)).astype(out.dtype)
                    copy(c, j).start()

    def slot(t):
        one_way(t, t - z, z == 0, lambda j: j > z, lambda k: nz - 1 - k,
                right_copy, r_out, r_in)
        one_way(t, t - (nz - 1 - z), z == nz - 1, lambda j: j < z, lambda k: k,
                left_copy, l_out, l_in)

    def store(c):
        if c < down_chunks:
            cols = slice(c * kv, (c + 1) * kv)
            return pltpu.make_async_copy(dg.at[:, cols], dg_h.at[:, cols], out_sem.at[HALVES + c])
        return pltpu.make_async_copy(ug, ug_h, out_sem.at[HALVES + c])

    def final(c):
        from_left = jnp.where(z > 0, r_in[c, z].astype(F32), 0.0)
        from_right = jnp.where(z < nz - 1, l_in[c, z].astype(F32), 0.0)
        total = own[c, z] + from_left + from_right
        if c < down_chunks:
            dg[:, c * kv : (c + 1) * kv] = total
        else:
            ug[...] = total
        store(c).start()

    def frozen(source, h, cols):
        at = pl.ds(pl.multiple_of(source * kv, LANES), kv)
        return lax.dot_general(dy[source, pl.ds(h * half, half), :], w[cols, at], LAST,
                               preferred_element_type=F32)

    pieces = 4
    piece = width // pieces

    def near(p):
        if p == 0:
            loads[4].wait()
            for h in range(HALVES):
                dy_copy(h, 0, partner, partner).wait_recv()
        cols = slice(p * piece, (p + 1) * piece)
        for h in range(HALVES):
            at = slice(h * half, (h + 1) * half)
            acc[at, cols] = (
                jnp.dot(ge[at, :], d[:, cols], preferred_element_type=F32)
                + frozen(me, h, cols) + frozen(partner, h, cols)
            )

    def forward(h):
        for off in range(1, chips):
            got = away(-off, core)
            dy_copy(h, off, got, got).wait_recv()
            dy_copy(h, chips - 1 + off, got, partner).start()
            if h + 1 < HALVES:
                dy_copy(h, off, me, away(off, core)).wait_send()
                dy_copy(h + 1, off, me, away(off, core)).start()

    def ig_store(h):
        at = pl.ds(h * half, half)
        return pltpu.make_async_copy(ig.at[at], ig_h.at[at], out_sem.at[h])

    def far(h):
        for off in range(1, chips):
            dy_copy(h, chips - 1 + off, away(-off, 1 - core), partner).wait_recv()

        @pl.loop(0, pieces)
        def _(p):
            at = pl.ds(h * half, half)
            cols = pl.ds(pl.multiple_of(p * piece, LANES), piece)
            total = acc[at, cols]
            for off in range(1, chips):
                for side in (0, 1):
                    total = total + frozen(away(-off, side), h, cols)
            ig[at, cols] = total.astype(BF16)

        ig_store(h).start()

    before = {0: [lambda: term(0)], 1: [lambda: term(1)], 2: [lambda: term(2)],
              5: [lambda: near(0)], 6: [lambda: near(1)], 7: [lambda: near(2)],
              8: [lambda: near(3)], 9: [lambda: forward(0)], 10: [lambda: far(0)],
              14: [lambda: forward(1)], 15: [lambda: far(1)]}
    before[3] = [lambda c=c: term(c) for c in range(3, down_chunks)]
    before[4] = [lambda: expand(1, ue_t, None), lambda: term(down_chunks)]

    expand(0, ge_t, ge)
    done = 0
    reached = 0
    for mark in range(17):
        upto = sends + 1 if mark == 16 else mark * sends // 15
        upto = min(upto, sends + 1)

        def run(lo, hi):
            if hi - lo == 1:
                slot(lo)
            elif hi > lo:
                lax.fori_loop(lo, hi, lambda t, _: (slot(t), 0)[1], 0)

        while reached < upto:
            stop = min(upto, (reached // steps + 1) * steps + 1 if reached % steps else reached + 1)
            if reached % steps:
                stop = min(upto, (reached // steps + 1) * steps)
            run(reached, stop)
            if (stop - 1) % steps == 0 and stop - 1 > 0:
                final((stop - 1) // steps - 1)
                done += 1
            reached = stop
        for work in before.get(mark, ()):
            work()

    for kind in range(2):
        for off in range(1, nt):
            part_copy(kind, off, me, me).wait_send()
            low_copy(kind, off, me).wait_send()
    for h in range(HALVES):
        dy_copy(h, 0, me, partner).wait_send()
        for off in range(1, chips):
            if h == HALVES - 1:
                dy_copy(h, off, me, away(off, core)).wait_send()
            dy_copy(h, chips - 1 + off, me, partner).wait_send()

    @pl.loop(0, sends)
    def _(i):
        c = i // steps
        k = lax.rem(i, steps)

        @pl.when((nz - 1 - k > z) & ((z > 0) | (i >= sends - WINDOW)))
        def _():
            right_copy(c, nz - 1 - k).wait_send()

        @pl.when((k < z) & ((z < nz - 1) | (i >= sends - WINDOW)))
        def _():
            left_copy(c, k).wait_send()

    for h in range(HALVES):
        ig_store(h).wait()
    for c in range(chunks):
        store(c).wait()


def body(stored_input, output_gradient, frozen_key_value, adapter_down_weight,
         adapter_up_weight, token_tenant, adapter_position):
    nt = lax.axis_size("tensor")
    nz = lax.axis_size("dp")
    rows, width = stored_input.shape
    kv = output_gradient.shape[1]
    adapters, rank = adapter_down_weight.shape[:2]
    ar = adapters * rank
    per = ar // nz
    chunks = width // kv + 1
    q = rows * rank // LANES // nt
    ways = nt - 1
    wire = BF16 if nz <= 4 else F32
    dma = pltpu.SemaphoreType.DMA
    hbm = pl.BlockSpec(memory_space=pl.ANY)
    ig, dg, ug = pl.pallas_call(
        functools.partial(kernel, nt, nz, rank),
        out_shape=(
            jax.ShapeDtypeStruct((rows, width), BF16),
            jax.ShapeDtypeStruct((per, width), F32),
            jax.ShapeDtypeStruct((per, kv), F32),
        ),
        in_specs=[hbm] * 5 + [pl.BlockSpec(memory_space=pltpu.VMEM),
                              pl.BlockSpec(memory_space=pltpu.SMEM)],
        out_specs=(hbm, hbm, hbm),
        scratch_shapes=[
            pltpu.VMEM((rows, width), BF16),
            pltpu.VMEM((nt, rows, kv), BF16),
            pltpu.VMEM(frozen_key_value.shape, BF16),
            pltpu.VMEM((ar, width), BF16),
            pltpu.VMEM((ar, kv), BF16),
            pltpu.VMEM((rows, LANES), F32),
            pltpu.VMEM((8, rows), F32),
            pltpu.VMEM((2, nt, q, LANES), F32),
            pltpu.VMEM((2, nt, q, LANES), F32),
            pltpu.VMEM((2, nt, q, LANES), BF16),
            pltpu.VMEM((rows, ar), BF16),
            pltpu.VMEM((ar, rows), BF16),
            pltpu.VMEM((ar, rows), BF16),
            pltpu.VMEM((chunks, nz, per, kv), F32),
            pltpu.VMEM((rows, width), F32),
            pltpu.VMEM((rows, width), BF16),
            pltpu.VMEM((chunks, nz, per, kv), wire),
            pltpu.VMEM((chunks, nz, per, kv), wire),
            pltpu.VMEM((chunks, nz, per, kv), wire),
            pltpu.VMEM((chunks, nz, per, kv), wire),
            pltpu.VMEM((per, width), F32),
            pltpu.VMEM((per, kv), F32),
            dma((5,)),
            dma((2, nt)), dma((2, nt)), dma((2, nt)), dma((2, nt)),
            dma((HALVES, ways)), dma((HALVES, ways)),
            dma((chunks, nz)), dma((chunks, nz)), dma((chunks, nz)), dma((chunks, nz)),
            dma((HALVES + chunks,)),
        ],
        compiler_params=pltpu.CompilerParams(
            collective_id=0, has_side_effects=True, vmem_limit_bytes=60 * 1024 * 1024
        ),
    )(
        stored_input, output_gradient, frozen_key_value,
        adapter_down_weight.reshape(ar, width), adapter_up_weight.reshape(ar, kv),
        token_tenant.reshape(rows // LANES, LANES), adapter_position,
    )
    return ig, dg.reshape(per // rank, rank, width), ug.reshape(per // rank, rank, kv)


def solution(mesh):
    in_specs = (
        P(("groups", "dp"), "tensor"),
        P(("groups", "dp"), "tensor"),
        P("tensor", None),
        P("groups", None, "tensor"),
        P("groups", None, "tensor"),
        P(("groups", "dp"), None),
        P("groups"),
    )
    out_specs = (
        P(("groups", "dp"), "tensor"),
        P(("groups", "dp"), None, "tensor"),
        P(("groups", "dp"), None, "tensor"),
    )
    return jax.shard_map(body, mesh=mesh, in_specs=in_specs, out_specs=out_specs, check_vma=False)
```

```python
import functools

import jax
import jax.numpy as jnp
from jax import lax
from jax.experimental import pallas as pl
from jax.experimental.pallas import tpu as pltpu
from jax.sharding import PartitionSpec as P

MESH = pl.DeviceIdType.MESH
F32 = jnp.float32
BF16 = jnp.bfloat16
LANES = 128
LAST = (((1,), (1,)), ((), ()))
HALVES = 2
WINDOW = 3
LAG = 3


def kernel(nt, nz, rank, x_h, dy_h, w_h, d_h, u_h, tt, pos, ig, dg, ug,
           x, dy, w, d, u, ab, a_t, packed, landed, low, ge, ge_t, ue_t, own, acc,
           r_out, r_in, l_out, l_in,
           load_sem, part_s, part_r, low_s, low_r, dy_s, dy_r, rs_s, rs_r, ls_s, ls_r):
    me = lax.axis_index("tensor")
    z = lax.axis_index("dp")
    rows, width = x.shape
    kv = dy.shape[2]
    ar = d.shape[0]
    per = ar // nz
    tiles = ar // LANES
    fold = LANES // rank
    chunk_rows = rows // fold
    down_chunks = width // kv
    chunks = down_chunks + 1
    half = rows // HALVES
    chips = nt // 2
    core = lax.rem(me, 2)
    chip = me // 2
    partner = chip * 2 + 1 - core

    loads = [
        pltpu.make_async_copy(src, dst, load_sem.at[i])
        for i, (src, dst) in enumerate(
            [(u_h, u), (dy_h, dy.at[me]), (d_h, d), (x_h, x), (w_h, w)]
        )
    ]
    loads[0].start()
    loads[1].start()

    barrier = pltpu.get_barrier_semaphore()
    for off in range(1, nt):
        pl.semaphore_signal(barrier, inc=1, device_id={"tensor": lax.rem(me + off, nt)},
                            device_id_type=MESH)

    @pl.when(z > 0)
    def _():
        pl.semaphore_signal(barrier, inc=1, device_id={"dp": z - 1}, device_id_type=MESH)

    @pl.when(z < nz - 1)
    def _():
        pl.semaphore_signal(barrier, inc=1, device_id={"dp": z + 1}, device_id_type=MESH)

    loads[3].start()
    loads[2].start()

    for i in range(rows // LANES):
        row = jnp.broadcast_to(tt[i : i + 1, :].astype(F32), (LANES, LANES))
        a_t[:, i * LANES : (i + 1) * LANES] = row[0:8, :]
        ab[i * LANES : (i + 1) * LANES, :] = row.T

    group_of = (lax.broadcasted_iota(jnp.int32, (chunk_rows, LANES), 1) // rank).astype(F32)
    group_t = (lax.broadcasted_iota(jnp.int32, (LANES, chunk_rows), 0) // rank).astype(F32)

    def spread(v):
        step = LANES // 2
        while step >= rank:
            v = v + pltpu.roll(v, step, 1)
            step //= 2
        return v

    def project(kind, source, weight):
        total = jnp.zeros((chunk_rows, LANES), F32)
        for k in range(fold):
            part = lax.dot_general(source(k), weight[...], LAST, preferred_element_type=F32)
            a_k = ab[k * chunk_rows : (k + 1) * chunk_rows, :]
            mine = jnp.zeros((chunk_rows, LANES), F32)
            for j in range(tiles):
                mine = mine + jnp.where(
                    a_k == group_of + float(fold * j), part[:, j * LANES : (j + 1) * LANES], 0.0
                )
            total = jnp.where(group_of == float(k), spread(mine), total)
        packed[kind] = total.reshape(packed.shape[1:])

    def part_copy(kind, off, src_slot, dst_slot):
        return pltpu.make_async_remote_copy(
            src_ref=packed.at[kind, src_slot], dst_ref=landed.at[kind, dst_slot],
            send_sem=part_s.at[kind, off], recv_sem=part_r.at[kind, off],
            device_id={"tensor": lax.rem(me + off, nt)}, device_id_type=MESH)

    def low_copy(kind, off, slot):
        return pltpu.make_async_remote_copy(
            src_ref=low.at[kind, slot], dst_ref=low.at[kind, slot],
            send_sem=low_s.at[kind, off], recv_sem=low_r.at[kind, off],
            device_id={"tensor": lax.rem(me + off, nt)}, device_id_type=MESH)

    def send_parts(kind):
        for off in range(1, nt):
            part_copy(kind, off, lax.rem(me + off, nt), me).start()

    def sum_parts(kind):
        total = packed[kind, me]
        for off in range(1, nt):
            sender = lax.rem(me + nt - off, nt)
            part_copy(kind, off, me, sender).wait_recv()
            total = total + landed[kind, sender]
        low[kind, me] = total.astype(BF16)
        for off in range(1, nt):
            low_copy(kind, off, me).start()

    def get_low(kind):
        for off in range(1, nt):
            low_copy(kind, off, lax.rem(me + nt - off, nt)).wait_recv()
        return low[kind].astype(F32).reshape(chunk_rows, LANES)

    def dy_copy(h, way, slot, to):
        block = dy.at[slot, pl.ds(h * half, half)]
        return pltpu.make_async_remote_copy(
            src_ref=block, dst_ref=block, send_sem=dy_s.at[h, way], recv_sem=dy_r.at[h, way],
            device_id={"tensor": to}, device_id_type=MESH)

    def away(off, side):
        return lax.rem(chip + off + chips, chips) * 2 + side

    loads[0].wait()
    loads[1].wait()
    project(0, lambda k: dy[me, k * chunk_rows : (k + 1) * chunk_rows, :], u)
    neighbours = (z > 0).astype(jnp.int32) + (z < nz - 1).astype(jnp.int32)
    pl.semaphore_wait(barrier, nt - 1 + neighbours)
    send_parts(0)
    loads[2].wait()
    loads[3].wait()
    project(1, lambda k: x[k * chunk_rows : (k + 1) * chunk_rows, :], d)
    send_parts(1)
    loads[4].start()

    home = jnp.zeros((8, rows), F32)
    for a in range(ar // rank):
        home = home + jnp.where(a_t[...] == float(a), pos[a].astype(F32), 0.0)

    sum_parts(0)
    for h in range(HALVES):
        dy_copy(h, 0, me, partner).start()

    def expand(kind, out_t):
        got = get_low(kind)
        for k in range(fold):
            at = slice(k * chunk_rows, (k + 1) * chunk_rows)
            rep = spread(jnp.where(group_of == float(k), got, 0.0))
            rep_t = rep.T
            home_k = jnp.broadcast_to(home[0:1, at], (LANES, chunk_rows))
            for j in range(tiles):
                cols = slice(j * LANES, (j + 1) * LANES)
                out_t[cols, at] = jnp.where(
                    home_k == group_t + float(fold * j), rep_t, 0.0).astype(BF16)

    def expand_rows():
        got = low[0].astype(F32).reshape(chunk_rows, LANES)
        for k in range(fold):
            at = slice(k * chunk_rows, (k + 1) * chunk_rows)
            rep = spread(jnp.where(group_of == float(k), got, 0.0))
            for j in range(tiles):
                ge[at, j * LANES : (j + 1) * LANES] = jnp.where(
                    ab[at, :] == group_of + float(fold * j), rep, 0.0).astype(BF16)

    def sum_u():
        sum_parts(1)
        for h in range(HALVES):
            for off in range(1, chips):
                dy_copy(h, off, me, away(off, core)).start()

    def term(c):
        if c < down_chunks:
            block = jnp.dot(ge_t[...], x[:, c * kv : (c + 1) * kv], preferred_element_type=F32)
        else:
            block = jnp.dot(ue_t[...], dy[me], preferred_element_type=F32)
        own[c] = block.reshape(nz, per, kv)

    steps = nz - 1
    sends = chunks * steps

    def right_copy(c, j):
        return pltpu.make_async_remote_copy(
            src_ref=r_out.at[c, j], dst_ref=r_in.at[c, j],
            send_sem=rs_s.at[c, j], recv_sem=rs_r.at[c, j],
            device_id={"dp": lax.rem(z + 1, nz)}, device_id_type=MESH)

    def left_copy(c, j):
        return pltpu.make_async_remote_copy(
            src_ref=l_out.at[c, j], dst_ref=l_in.at[c, j],
            send_sem=ls_s.at[c, j], recv_sem=ls_r.at[c, j],
            device_id={"dp": lax.rem(z + nz - 1, nz)}, device_id_type=MESH)

    def one_way(t, index, first, farther, owner_of, copy, out, inn):
        c = index // steps
        j = owner_of(lax.rem(index, steps))

        @pl.when((index >= 0) & (index < sends))
        def _():
            @pl.when(first)
            def _():
                @pl.when(index >= WINDOW)
                def _():
                    back = index - WINDOW
                    copy(back // steps, owner_of(lax.rem(back, steps))).wait_send()

                out[c, j] = own[c, j].astype(out.dtype)
                copy(c, j).start()

            @pl.when(jnp.logical_not(first))
            def _():
                @pl.when(farther(j))
                def _():
                    copy(c, j).wait_recv()
                    out[c, j] = (own[c, j] + inn[c, j].astype(F32)).astype(out.dtype)
                    copy(c, j).start()

    def slot(t):
        one_way(t, t - LAG * z, z == 0, lambda j: j > z, lambda k: nz - 1 - k,
                right_copy, r_out, r_in)
        one_way(t, t - LAG * (nz - 1 - z), z == nz - 1, lambda j: j < z, lambda k: k,
                left_copy, l_out, l_in)

    def final(c):
        @pl.when(z > 0)
        def _():
            right_copy(c, z).wait_recv()

        @pl.when(z < nz - 1)
        def _():
            left_copy(c, z).wait_recv()

        from_left = jnp.where(z > 0, r_in[c, z].astype(F32), 0.0)
        from_right = jnp.where(z < nz - 1, l_in[c, z].astype(F32), 0.0)
        total = own[c, z] + from_left + from_right
        if c < down_chunks:
            dg[:, c * kv : (c + 1) * kv] = total
        else:
            ug[...] = total

    def frozen(source, h, cols):
        at = pl.ds(pl.multiple_of(source * kv, LANES), kv)
        return lax.dot_general(dy[source, pl.ds(h * half, half), :], w[cols, at], LAST,
                               preferred_element_type=F32)

    pieces = 4
    piece = width // pieces

    def near(p):
        if p == 0:
            loads[4].wait()
            for h in range(HALVES):
                dy_copy(h, 0, partner, partner).wait_recv()
        cols = slice(p * piece, (p + 1) * piece)
        for h in range(HALVES):
            at = slice(h * half, (h + 1) * half)
            acc[at, cols] = (
                jnp.dot(ge[at, :], d[:, cols], preferred_element_type=F32)
                + frozen(me, h, cols) + frozen(partner, h, cols)
            )

    def forward(h):
        for off in range(1, chips):
            got = away(-off, core)
            dy_copy(h, off, got, got).wait_recv()
            dy_copy(h, chips - 1 + off, got, partner).start()

    def far(h):
        for off in range(1, chips):
            dy_copy(h, chips - 1 + off, away(-off, 1 - core), partner).wait_recv()

        @pl.loop(0, pieces)
        def _(p):
            at = pl.ds(h * half, half)
            cols = pl.ds(pl.multiple_of(p * piece, LANES), piece)
            total = acc[at, cols]
            for off in range(1, chips):
                for side in (0, 1):
                    total = total + frozen(away(-off, side), h, cols)
            ig[at, cols] = total.astype(BF16)


    before = {0: [lambda: term(0)], 1: [sum_u, lambda: term(1)],
              3: [expand_rows],
              4: [lambda: expand(1, ue_t), lambda: term(down_chunks)],
              5: [lambda: near(0)], 6: [lambda: near(1)],
              7: [lambda: near(2)], 8: [lambda: near(3), lambda: forward(0)], 10: [lambda: far(0)],
              12: [lambda: forward(1)], 15: [lambda: far(1)]}
    before[2] = [lambda c=c: term(c) for c in range(2, down_chunks)]

    expand(0, ge_t)
    reached = 0
    slots = max(sends, (chunks - 1) * steps + LAG * (nz - 2) + 1)
    for mark in range(17):
        upto = slots if mark == 16 else mark * sends // 15
        if upto - reached == 1:
            slot(reached)
        elif upto > reached:
            lax.fori_loop(reached, upto, lambda t, _: (slot(t), 0)[1], 0)
        reached = upto
        for work in before.get(mark, ()):
            work()

    for c in range(chunks):
        final(c)

    for kind in range(2):
        for off in range(1, nt):
            part_copy(kind, off, me, me).wait_send()
            low_copy(kind, off, me).wait_send()
    for h in range(HALVES):
        dy_copy(h, 0, me, partner).wait_send()
        for off in range(1, chips):
            dy_copy(h, off, me, away(off, core)).wait_send()
            dy_copy(h, chips - 1 + off, me, partner).wait_send()

    @pl.loop(0, sends)
    def _(i):
        c = i // steps
        k = lax.rem(i, steps)

        @pl.when((nz - 1 - k > z) & ((z > 0) | (i >= sends - WINDOW)))
        def _():
            right_copy(c, nz - 1 - k).wait_send()

        @pl.when((k < z) & ((z < nz - 1) | (i >= sends - WINDOW)))
        def _():
            left_copy(c, k).wait_send()


def body(stored_input, output_gradient, frozen_key_value, adapter_down_weight,
         adapter_up_weight, token_tenant, adapter_position):
    nt = lax.axis_size("tensor")
    nz = lax.axis_size("dp")
    rows, width = stored_input.shape
    kv = output_gradient.shape[1]
    adapters, rank = adapter_down_weight.shape[:2]
    ar = adapters * rank
    per = ar // nz
    chunks = width // kv + 1
    q = rows * rank // LANES // nt
    ways = nt - 1
    wire = BF16 if nz <= 4 else F32
    dma = pltpu.SemaphoreType.DMA
    hbm = pl.BlockSpec(memory_space=pl.ANY)
    ig, dg, ug = pl.pallas_call(
        functools.partial(kernel, nt, nz, rank),
        out_shape=(
            pltpu.VMEM((rows, width), BF16),
            pltpu.VMEM((per, width), F32),
            pltpu.VMEM((per, kv), F32),
        ),
        in_specs=[hbm] * 5 + [pl.BlockSpec(memory_space=pltpu.VMEM),
                              pl.BlockSpec(memory_space=pltpu.SMEM)],
        out_specs=(pl.BlockSpec(memory_space=pltpu.VMEM),) * 3,
        scratch_shapes=[
            pltpu.VMEM((rows, width), BF16),
            pltpu.VMEM((nt, rows, kv), BF16),
            pltpu.VMEM(frozen_key_value.shape, BF16),
            pltpu.VMEM((ar, width), BF16),
            pltpu.VMEM((ar, kv), BF16),
            pltpu.VMEM((rows, LANES), F32),
            pltpu.VMEM((8, rows), F32),
            pltpu.VMEM((2, nt, q, LANES), F32),
            pltpu.VMEM((2, nt, q, LANES), F32),
            pltpu.VMEM((2, nt, q, LANES), BF16),
            pltpu.VMEM((rows, ar), BF16),
            pltpu.VMEM((ar, rows), BF16),
            pltpu.VMEM((ar, rows), BF16),
            pltpu.VMEM((chunks, nz, per, kv), F32),
            pltpu.VMEM((rows, width), F32),
            pltpu.VMEM((chunks, nz, per, kv), wire),
            pltpu.VMEM((chunks, nz, per, kv), wire),
            pltpu.VMEM((chunks, nz, per, kv), wire),
            pltpu.VMEM((chunks, nz, per, kv), wire),
            dma((5,)),
            dma((2, nt)), dma((2, nt)), dma((2, nt)), dma((2, nt)),
            dma((HALVES, ways)), dma((HALVES, ways)),
            dma((chunks, nz)), dma((chunks, nz)), dma((chunks, nz)), dma((chunks, nz)),
        ],
        compiler_params=pltpu.CompilerParams(
            collective_id=0, has_side_effects=True, vmem_limit_bytes=52 * 1024 * 1024
        ),
    )(
        stored_input, output_gradient, frozen_key_value,
        adapter_down_weight.reshape(ar, width), adapter_up_weight.reshape(ar, kv),
        token_tenant.reshape(rows // LANES, LANES), adapter_position,
    )
    return ig, dg.reshape(per // rank, rank, width), ug.reshape(per // rank, rank, kv)


def solution(mesh):
    in_specs = (
        P(("groups", "dp"), "tensor"),
        P(("groups", "dp"), "tensor"),
        P("tensor", None),
        P("groups", None, "tensor"),
        P("groups", None, "tensor"),
        P(("groups", "dp"), None),
        P("groups"),
    )
    out_specs = (
        P(("groups", "dp"), "tensor"),
        P(("groups", "dp"), None, "tensor"),
        P(("groups", "dp"), None, "tensor"),
    )
    return jax.shard_map(body, mesh=mesh, in_specs=in_specs, out_specs=out_specs, check_vma=False)
```

```python
import functools

import jax
import jax.numpy as jnp
from jax import lax
from jax.experimental import pallas as pl
from jax.experimental.pallas import tpu as pltpu
from jax.sharding import PartitionSpec as P

MESH = pl.DeviceIdType.MESH
F32 = jnp.float32
BF16 = jnp.bfloat16
LANES = 128
LAST = (((1,), (1,)), ((), ()))
HALVES = 2
WINDOW = 3
LAG = 2


def kernel(nt, nz, rank, x_h, dy_h, w_h, d_h, u_h, tt, pos, ig, dg, ug,
           x, dy, w, d, u, ab, a_t, packed, landed, low, ge, ge_t, ue_t, own, acc,
           r_out, r_in, l_out, l_in,
           load_sem, part_s, part_r, low_s, low_r, dy_s, dy_r, rs_s, rs_r, ls_s, ls_r):
    me = lax.axis_index("tensor")
    z = lax.axis_index("dp")
    rows, width = x.shape
    kv = dy.shape[2]
    ar = d.shape[0]
    per = ar // nz
    tiles = ar // LANES
    fold = LANES // rank
    chunk_rows = rows // fold
    down_chunks = width // kv
    chunks = down_chunks + 1
    half = rows // HALVES
    chips = nt // 2
    core = lax.rem(me, 2)
    chip = me // 2
    partner = chip * 2 + 1 - core

    loads = [
        pltpu.make_async_copy(src, dst, load_sem.at[i])
        for i, (src, dst) in enumerate(
            [(u_h, u), (dy_h, dy.at[me]), (d_h, d), (x_h, x), (w_h, w)]
        )
    ]
    loads[0].start()
    loads[1].start()

    barrier = pltpu.get_barrier_semaphore()
    for off in range(1, nt):
        pl.semaphore_signal(barrier, inc=1, device_id={"tensor": lax.rem(me + off, nt)},
                            device_id_type=MESH)

    @pl.when(z > 0)
    def _():
        pl.semaphore_signal(barrier, inc=1, device_id={"dp": z - 1}, device_id_type=MESH)

    @pl.when(z < nz - 1)
    def _():
        pl.semaphore_signal(barrier, inc=1, device_id={"dp": z + 1}, device_id_type=MESH)

    loads[3].start()
    loads[2].start()

    for i in range(rows // LANES):
        row = jnp.broadcast_to(tt[i : i + 1, :].astype(F32), (LANES, LANES))
        a_t[:, i * LANES : (i + 1) * LANES] = row[0:8, :]
        ab[i * LANES : (i + 1) * LANES, :] = row.T

    group_of = (lax.broadcasted_iota(jnp.int32, (chunk_rows, LANES), 1) // rank).astype(F32)
    group_t = (lax.broadcasted_iota(jnp.int32, (LANES, chunk_rows), 0) // rank).astype(F32)

    def spread(v):
        step = LANES // 2
        while step >= rank:
            v = v + pltpu.roll(v, step, 1)
            step //= 2
        return v

    def project(kind, source, weight):
        total = jnp.zeros((chunk_rows, LANES), F32)
        for k in range(fold):
            part = lax.dot_general(source(k), weight[...], LAST, preferred_element_type=F32)
            a_k = ab[k * chunk_rows : (k + 1) * chunk_rows, :]
            mine = jnp.zeros((chunk_rows, LANES), F32)
            for j in range(tiles):
                mine = mine + jnp.where(
                    a_k == group_of + float(fold * j), part[:, j * LANES : (j + 1) * LANES], 0.0
                )
            total = jnp.where(group_of == float(k), spread(mine), total)
        packed[kind] = total.reshape(packed.shape[1:])

    def part_copy(kind, off, src_slot, dst_slot):
        return pltpu.make_async_remote_copy(
            src_ref=packed.at[kind, src_slot], dst_ref=landed.at[kind, dst_slot],
            send_sem=part_s.at[kind, off], recv_sem=part_r.at[kind, off],
            device_id={"tensor": lax.rem(me + off, nt)}, device_id_type=MESH)

    def low_copy(kind, off, slot):
        return pltpu.make_async_remote_copy(
            src_ref=low.at[kind, slot], dst_ref=low.at[kind, slot],
            send_sem=low_s.at[kind, off], recv_sem=low_r.at[kind, off],
            device_id={"tensor": lax.rem(me + off, nt)}, device_id_type=MESH)

    def send_parts(kind):
        for off in range(1, nt):
            part_copy(kind, off, lax.rem(me + off, nt), me).start()

    def sum_parts(kind):
        total = packed[kind, me]
        for off in range(1, nt):
            sender = lax.rem(me + nt - off, nt)
            part_copy(kind, off, me, sender).wait_recv()
            total = total + landed[kind, sender]
        low[kind, me] = total.astype(BF16)
        for off in range(1, nt):
            low_copy(kind, off, me).start()

    def get_low(kind):
        for off in range(1, nt):
            low_copy(kind, off, lax.rem(me + nt - off, nt)).wait_recv()
        return low[kind].astype(F32).reshape(chunk_rows, LANES)

    def dy_copy(h, way, slot, to):
        block = dy.at[slot, pl.ds(h * half, half)]
        return pltpu.make_async_remote_copy(
            src_ref=block, dst_ref=block, send_sem=dy_s.at[h, way], recv_sem=dy_r.at[h, way],
            device_id={"tensor": to}, device_id_type=MESH)

    def away(off, side):
        return lax.rem(chip + off + chips, chips) * 2 + side

    loads[0].wait()
    loads[1].wait()
    project(0, lambda k: dy[me, k * chunk_rows : (k + 1) * chunk_rows, :], u)
    neighbours = (z > 0).astype(jnp.int32) + (z < nz - 1).astype(jnp.int32)
    pl.semaphore_wait(barrier, nt - 1 + neighbours)
    send_parts(0)
    loads[2].wait()
    loads[3].wait()
    project(1, lambda k: x[k * chunk_rows : (k + 1) * chunk_rows, :], d)
    send_parts(1)
    loads[4].start()

    home = jnp.zeros((8, rows), F32)
    for a in range(ar // rank):
        home = home + jnp.where(a_t[...] == float(a), pos[a].astype(F32), 0.0)

    sum_parts(0)
    for h in range(HALVES):
        dy_copy(h, 0, me, partner).start()

    def expand(kind, out_t):
        got = get_low(kind)
        for k in range(fold):
            at = slice(k * chunk_rows, (k + 1) * chunk_rows)
            rep = spread(jnp.where(group_of == float(k), got, 0.0))
            rep_t = rep.T
            home_k = jnp.broadcast_to(home[0:1, at], (LANES, chunk_rows))
            for j in range(tiles):
                cols = slice(j * LANES, (j + 1) * LANES)
                out_t[cols, at] = jnp.where(
                    home_k == group_t + float(fold * j), rep_t, 0.0).astype(BF16)

    def expand_rows():
        got = low[0].astype(F32).reshape(chunk_rows, LANES)
        for k in range(fold):
            at = slice(k * chunk_rows, (k + 1) * chunk_rows)
            rep = spread(jnp.where(group_of == float(k), got, 0.0))
            for j in range(tiles):
                ge[at, j * LANES : (j + 1) * LANES] = jnp.where(
                    ab[at, :] == group_of + float(fold * j), rep, 0.0).astype(BF16)

    def sum_u():
        sum_parts(1)
        for h in range(HALVES):
            for off in range(1, chips):
                dy_copy(h, off, me, away(off, core)).start()

    def term(c):
        if c < down_chunks:
            block = jnp.dot(ge_t[...], x[:, c * kv : (c + 1) * kv], preferred_element_type=F32)
        else:
            block = jnp.dot(ue_t[...], dy[me], preferred_element_type=F32)
        own[c] = block.reshape(nz, per, kv)

    steps = nz - 1
    sends = chunks * steps

    def right_copy(c, j):
        return pltpu.make_async_remote_copy(
            src_ref=r_out.at[c, j], dst_ref=r_in.at[c, j],
            send_sem=rs_s.at[c, j], recv_sem=rs_r.at[c, j],
            device_id={"dp": lax.rem(z + 1, nz)}, device_id_type=MESH)

    def left_copy(c, j):
        return pltpu.make_async_remote_copy(
            src_ref=l_out.at[c, j], dst_ref=l_in.at[c, j],
            send_sem=ls_s.at[c, j], recv_sem=ls_r.at[c, j],
            device_id={"dp": lax.rem(z + nz - 1, nz)}, device_id_type=MESH)

    def one_way(t, index, first, farther, owner_of, copy, out, inn):
        c = index // steps
        j = owner_of(lax.rem(index, steps))

        @pl.when((index >= 0) & (index < sends))
        def _():
            @pl.when(first)
            def _():
                @pl.when(index >= WINDOW)
                def _():
                    back = index - WINDOW
                    copy(back // steps, owner_of(lax.rem(back, steps))).wait_send()

                out[c, j] = own[c, j].astype(out.dtype)
                copy(c, j).start()

            @pl.when(jnp.logical_not(first))
            def _():
                @pl.when(farther(j))
                def _():
                    copy(c, j).wait_recv()
                    out[c, j] = (own[c, j] + inn[c, j].astype(F32)).astype(out.dtype)
                    copy(c, j).start()

    def slot(t):
        one_way(t, t - LAG * z, z == 0, lambda j: j > z, lambda k: nz - 1 - k,
                right_copy, r_out, r_in)
        one_way(t, t - LAG * (nz - 1 - z), z == nz - 1, lambda j: j < z, lambda k: k,
                left_copy, l_out, l_in)

    def final(c):
        @pl.when(z > 0)
        def _():
            right_copy(c, z).wait_recv()

        @pl.when(z < nz - 1)
        def _():
            left_copy(c, z).wait_recv()

        from_left = jnp.where(z > 0, r_in[c, z].astype(F32), 0.0)
        from_right = jnp.where(z < nz - 1, l_in[c, z].astype(F32), 0.0)
        total = own[c, z] + from_left + from_right
        if c < down_chunks:
            dg[:, c * kv : (c + 1) * kv] = total
        else:
            ug[...] = total

    def frozen(source, h, cols):
        at = pl.ds(pl.multiple_of(source * kv, LANES), kv)
        return lax.dot_general(dy[source, pl.ds(h * half, half), :], w[cols, at], LAST,
                               preferred_element_type=F32)

    pieces = 4
    piece = width // pieces

    def near(p):
        if p == 0:
            loads[4].wait()
            for h in range(HALVES):
                dy_copy(h, 0, partner, partner).wait_recv()
        cols = slice(p * piece, (p + 1) * piece)
        for h in range(HALVES):
            at = slice(h * half, (h + 1) * half)
            acc[at, cols] = (
                jnp.dot(ge[at, :], d[:, cols], preferred_element_type=F32)
                + frozen(me, h, cols) + frozen(partner, h, cols)
            )

    def forward(h):
        for off in range(1, chips):
            got = away(-off, core)
            dy_copy(h, off, got, got).wait_recv()
            dy_copy(h, chips - 1 + off, got, partner).start()

    def far(h):
        for off in range(1, chips):
            dy_copy(h, chips - 1 + off, away(-off, 1 - core), partner).wait_recv()

        @pl.loop(0, pieces)
        def _(p):
            at = pl.ds(h * half, half)
            cols = pl.ds(pl.multiple_of(p * piece, LANES), piece)
            total = acc[at, cols]
            for off in range(1, chips):
                for side in (0, 1):
                    total = total + frozen(away(-off, side), h, cols)
            ig[at, cols] = total.astype(BF16)


    before = {0: [lambda: term(0), sum_u], 1: [lambda: term(1)],
              3: [expand_rows],
              4: [lambda: expand(1, ue_t), lambda: term(down_chunks)],
              5: [lambda: near(0)], 6: [lambda: near(1)],
              7: [lambda: near(2)], 8: [lambda: near(3), lambda: forward(0)], 10: [lambda: far(0)],
              12: [lambda: forward(1)], 15: [lambda: far(1)]}
    before[2] = [lambda c=c: term(c) for c in range(2, down_chunks)]

    expand(0, ge_t)
    reached = 0
    slots = max(sends, (chunks - 1) * steps + LAG * (nz - 2) + 1)
    for mark in range(17):
        upto = slots if mark == 16 else mark * sends // 15
        if upto - reached == 1:
            slot(reached)
        elif upto > reached:
            lax.fori_loop(reached, upto, lambda t, _: (slot(t), 0)[1], 0)
        reached = upto
        for work in before.get(mark, ()):
            work()

    for c in range(chunks):
        final(c)

    for kind in range(2):
        for off in range(1, nt):
            part_copy(kind, off, me, me).wait_send()
            low_copy(kind, off, me).wait_send()
    for h in range(HALVES):
        dy_copy(h, 0, me, partner).wait_send()
        for off in range(1, chips):
            dy_copy(h, off, me, away(off, core)).wait_send()
            dy_copy(h, chips - 1 + off, me, partner).wait_send()

    @pl.loop(0, sends)
    def _(i):
        c = i // steps
        k = lax.rem(i, steps)

        @pl.when((nz - 1 - k > z) & ((z > 0) | (i >= sends - WINDOW)))
        def _():
            right_copy(c, nz - 1 - k).wait_send()

        @pl.when((k < z) & ((z < nz - 1) | (i >= sends - WINDOW)))
        def _():
            left_copy(c, k).wait_send()


def body(stored_input, output_gradient, frozen_key_value, adapter_down_weight,
         adapter_up_weight, token_tenant, adapter_position):
    nt = lax.axis_size("tensor")
    nz = lax.axis_size("dp")
    rows, width = stored_input.shape
    kv = output_gradient.shape[1]
    adapters, rank = adapter_down_weight.shape[:2]
    ar = adapters * rank
    per = ar // nz
    chunks = width // kv + 1
    q = rows * rank // LANES // nt
    ways = nt - 1
    wire = BF16 if nz <= 4 else F32
    dma = pltpu.SemaphoreType.DMA
    hbm = pl.BlockSpec(memory_space=pl.ANY)
    ig, dg, ug = pl.pallas_call(
        functools.partial(kernel, nt, nz, rank),
        out_shape=(
            pltpu.VMEM((rows, width), BF16),
            pltpu.VMEM((per, width), F32),
            pltpu.VMEM((per, kv), F32),
        ),
        in_specs=[hbm] * 5 + [pl.BlockSpec(memory_space=pltpu.VMEM),
                              pl.BlockSpec(memory_space=pltpu.SMEM)],
        out_specs=(pl.BlockSpec(memory_space=pltpu.VMEM),) * 3,
        scratch_shapes=[
            pltpu.VMEM((rows, width), BF16),
            pltpu.VMEM((nt, rows, kv), BF16),
            pltpu.VMEM(frozen_key_value.shape, BF16),
            pltpu.VMEM((ar, width), BF16),
            pltpu.VMEM((ar, kv), BF16),
            pltpu.VMEM((rows, LANES), F32),
            pltpu.VMEM((8, rows), F32),
            pltpu.VMEM((2, nt, q, LANES), F32),
            pltpu.VMEM((2, nt, q, LANES), F32),
            pltpu.VMEM((2, nt, q, LANES), BF16),
            pltpu.VMEM((rows, ar), BF16),
            pltpu.VMEM((ar, rows), BF16),
            pltpu.VMEM((ar, rows), BF16),
            pltpu.VMEM((chunks, nz, per, kv), F32),
            pltpu.VMEM((rows, width), F32),
            pltpu.VMEM((chunks, nz, per, kv), wire),
            pltpu.VMEM((chunks, nz, per, kv), wire),
            pltpu.VMEM((chunks, nz, per, kv), wire),
            pltpu.VMEM((chunks, nz, per, kv), wire),
            dma((5,)),
            dma((2, nt)), dma((2, nt)), dma((2, nt)), dma((2, nt)),
            dma((HALVES, ways)), dma((HALVES, ways)),
            dma((chunks, nz)), dma((chunks, nz)), dma((chunks, nz)), dma((chunks, nz)),
        ],
        compiler_params=pltpu.CompilerParams(
            collective_id=0, has_side_effects=True, vmem_limit_bytes=52 * 1024 * 1024
        ),
    )(
        stored_input, output_gradient, frozen_key_value,
        adapter_down_weight.reshape(ar, width), adapter_up_weight.reshape(ar, kv),
        token_tenant.reshape(rows // LANES, LANES), adapter_position,
    )
    return ig, dg.reshape(per // rank, rank, width), ug.reshape(per // rank, rank, kv)


def solution(mesh):
    in_specs = (
        P(("groups", "dp"), "tensor"),
        P(("groups", "dp"), "tensor"),
        P("tensor", None),
        P("groups", None, "tensor"),
        P("groups", None, "tensor"),
        P(("groups", "dp"), None),
        P("groups"),
    )
    out_specs = (
        P(("groups", "dp"), "tensor"),
        P(("groups", "dp"), None, "tensor"),
        P(("groups", "dp"), None, "tensor"),
    )
    return jax.shard_map(body, mesh=mesh, in_specs=in_specs, out_specs=out_specs, check_vma=False)
```
